32 devices in a mesh: dp: 2 (over y), ctx: 4 (over x, core), tp: 4 (over z).
Axes of the slice: x: 2, y: 2, z: 4, core: 2. Of those that a mesh axis runs over, the one named last changes fastest.
Arguments:
- queries: bfloat16 [8, 512, 4096], P(('dp', 'ctx'), None, 'tp'), may hold values from -400 to 400
- key_rows: bfloat16 [8, 512, 1024], P(('dp', 'ctx'), None, 'tp'), may hold values from -6 to 6
- value_rows: bfloat16 [8, 512, 1024], P(('dp', 'ctx'), None, 'tp'), may hold values from -6 to 6
- out_grad: bfloat16 [8, 512, 4096], P(('dp', 'ctx'), None, 'tp'), may hold values from -6 to 6
- inputs: bfloat16 [8, 512, 8192], P(('dp', 'ctx'), None, 'tp'), may hold values from -0.125 to 0.125
- doc_lengths: int32 [8, 4], P('dp'), may hold values from 1 to 160, 512 in all within a row
- doc_plan: int32 [8, 4], P('dp'), may hold values from 0 to 3, each once within a row
Outputs:
- query_grad: bfloat16 [8, 640, 4096], P(('dp', 'ctx'), None, 'tp')
- key_grad: bfloat16 [8, 640, 1024], P(('dp', 'ctx'), None, 'tp')
- value_grad: bfloat16 [8, 640, 1024], P(('dp', 'ctx'), None, 'tp')
- weight_grad: float32 [8192, 1024], P(('tp', 'dp', 'ctx'))
The draws below stay inside these ranges and needn't reach their ends.
Inputs may be any that keep to these rules, and one draw needn't show every extreme that they name: `doc_lengths`: each row sums to 512; every document has at most 160 tokens, and one of each row has exactly 160. Each row is a permutation: document d of sequence s goes to context index doc_plan[s, d] of the same data group.
All inputs are finite; a program needn't handle non-finite values.
Results may differ from the reference program's by a relative error of at most 0.012.
Values may be sent and summed in bfloat16 or wider, within the bound.
A program may use at most 64 MiB of HBM per device.

```python
import math
import jax
import jax.numpy as jnp
import numpy as np
from jax import lax

D = 8192
HEADS = 32
KVH = 8
HD = 128
L = 512
NDOC = 4
CAP = 160
RECV = 640
SEQS = 8


def pair_draw(key):
    group_size = HEADS // KVH
    base_key = jax.random.fold_in(key, 71)
    key_first, key_second = jax.random.split(base_key, 2)
    keys_raw = jnp.clip(jax.random.normal(key_first, (SEQS, L, KVH, HD), jnp.float32), -6.0, 6.0)
    query_raw = jnp.clip(jax.random.normal(key_second, (SEQS, L, KVH, group_size, HD), jnp.float32), -6.0, 6.0)
    keys_out = keys_raw
    query_out = query_raw
    return (query_out.reshape(SEQS, L, HEADS * HD), keys_out.reshape(SEQS, L, KVH * HD))


def draw_queries(key, part):
    return pair_draw(key)[0].astype(jnp.bfloat16)


def draw_key_rows(key, part):
    return pair_draw(key)[1].astype(jnp.bfloat16)


def with_spikes(array, own_key, source, target, blocks, factor):
    owner, partner = [(jnp.arange(array.shape[axis_at]) // (array.shape[axis_at] // blocks)).reshape([-1 if axis == axis_at else 1 for axis in range(array.ndim)]) for axis_at in (source, target)]
    chosen = jax.random.permutation(own_key, blocks)[partner]
    strong = (owner == chosen) | (owner == (partner + blocks // 2) % blocks)
    return jnp.where(strong, factor * array, array)


def steps_of(stream_key, dims, pieces, low, high):
    loudness = 1.0
    for dim, shards_of in pieces:
        heights = jax.random.uniform(jax.random.fold_in(jax.random.fold_in(stream_key, 6), dim), (shards_of,), jnp.float32, low / len(pieces), high / len(pieces))
        loudness = loudness * jnp.repeat(jnp.exp(heights), dims[dim] // shards_of).reshape((-1,) + (1,) * (len(dims) - 1 - dim))
    return loudness


def split_up(amount, total, reach, lean):
    weights = [(1 << 20) // math.isqrt(grade ** lean) + 1 for grade in range(2, amount + 1)]
    rest, counts = total - reach - (amount - 1), [1] * (amount - 1)
    while rest > 0:
        movable = [i for i in range(amount - 1) if counts[i] < reach]
        mass, budget = sum([weights[i] for i in movable]), rest
        for i in movable:
            addition = min(reach - counts[i], max(1, budget * weights[i] // mass), rest)
            counts[i] = counts[i] + addition
            rest = rest - addition
    return np.array([reach] + counts)


def ragged(key, number_of, total, reach, skew):
    if number_of == 2:
        one = jax.random.randint(key, (), max(1, total - reach), min(reach, total - 1) + 1)
        return jnp.stack([one, total - one])
    tallies = jnp.asarray(split_up(number_of, total, reach, skew), jnp.int32)
    pairs = (number_of - 1) // 2
    donor, receiver = tallies[1:1 + 2 * pairs:2], tallies[2:2 + 2 * pairs:2]
    slack = jnp.minimum(donor - 1, reach - receiver)
    moved = jax.random.randint(jax.random.fold_in(key, 1), (pairs,), 0, 1 << 20) % (slack + 1)
    tallies = tallies.at[1:1 + 2 * pairs:2].set(donor - moved).at[2:2 + 2 * pairs:2].set(receiver + moved)
    return tallies[jax.random.permutation(jax.random.fold_in(key, 2), number_of)]


def gaussian(own_key, extent, width, reach, cuts=(), held_as=jnp.bfloat16):
    gain = steps_of(own_key, extent, cuts, -0.22, 0.18) if cuts else 1.0
    entries = jax.random.normal(own_key, extent, jnp.float32) * width * gain
    return jnp.minimum(jnp.maximum(entries, -reach), reach).astype(held_as)


def bell_draw_with(rng, dims, deviation, limit, shards, heavy, kind=jnp.bfloat16):
    entries = deviation * jax.random.normal(rng, dims, jnp.float32)
    if shards:
        entries = entries * steps_of(rng, dims, shards, -0.22, 0.18)
    return jnp.clip(with_spikes(entries, jax.random.fold_in(rng, 3), *heavy), -limit, limit).astype(kind)


def setup_inputs(seed: int = 0) -> dict:
    key_of = jax.random.split(jax.random.key(seed), 8)
    return {
        "queries": draw_queries(jax.random.fold_in(key_of[7], 71), 0),
        "key_rows": draw_key_rows(jax.random.fold_in(key_of[7], 71), 0),
        "value_rows": gaussian(key_of[2], (SEQS, L, KVH * HD), 1.0, 6.0, ((0, 8), (2, 4))),
        "out_grad": gaussian(key_of[3], (SEQS, L, HEADS * HD), 1.0, 6.0, ((0, 8), (2, 4))),
        "inputs": bell_draw_with(key_of[4], (SEQS, L, D), (1.0 / (SEQS * L) ** 0.5), 0.125, ((0, 8), (2, 4)), (0, 2, 8, 2.0)),
        "doc_lengths": jax.vmap(lambda own: ragged(own, NDOC, L, CAP, 2))(jax.random.split(key_of[5], SEQS)).reshape((SEQS, NDOC)).astype(jnp.int32),
        "doc_plan": jax.vmap(lambda own: jax.random.permutation(own, NDOC))(jax.random.split(key_of[6], SEQS)).reshape((SEQS, NDOC)).astype(jnp.int32),
    }


def block_grads(query_rows, key_part, value_part, grad_rows, allowed):
    score_scale = HD ** -0.5
    highest = lax.Precision.HIGHEST
    scores = jnp.einsum('nrcgh,nsch->ncgrs', query_rows, key_part, precision=highest) * score_scale
    scores = jnp.where(allowed[:, None, None, :, :] == 1, scores, -jnp.inf)
    largest = jnp.max(scores, axis=4, keepdims=True)
    raised = jnp.exp(scores - largest)
    weights = raised / jnp.sum(raised, axis=4, keepdims=True)
    weights_low = lax.optimization_barrier(weights.astype(jnp.bfloat16)).astype(jnp.float32)
    attended = jnp.einsum('ncgrs,nsch->nrcgh', weights_low, value_part, precision=highest)
    row_delta = jnp.einsum('nrcgh,nrcgh->ncgr', grad_rows, attended, precision=highest)
    prob_grad = jnp.einsum('nrcgh,nsch->ncgrs', grad_rows, value_part, precision=highest)
    dscore = (weights * (prob_grad - row_delta[..., None])).astype(jnp.bfloat16)
    dscore = lax.optimization_barrier(dscore).astype(jnp.float32)
    query_grad = jnp.einsum('ncgrs,nsch->nrcgh', dscore, key_part, precision=highest) * score_scale
    key_grad = jnp.einsum('ncgrs,nrcgh->nsch', dscore, query_rows, precision=highest) * score_scale
    value_grad = jnp.einsum('ncgrs,nrcgh->nsch', weights_low, grad_rows, precision=highest)
    return query_grad, key_grad, value_grad


def reference(queries, key_rows, value_rows, out_grad, inputs, doc_lengths, doc_plan):
    group_size = HEADS // KVH
    starts = jnp.cumsum(doc_lengths, axis=1) - doc_lengths
    doc_ids = jnp.arange(NDOC, dtype=jnp.int32)
    matches = (doc_plan[:, None, :] == doc_ids[None, :, None]).astype(jnp.int32)
    inverse = jnp.sum(doc_ids[None, None, :] * matches, axis=2).astype(jnp.int32)
    offsets = jnp.arange(CAP, dtype=jnp.int32)
    causal = offsets[None, :] <= offsets[:, None]
    diagonal = offsets[None, :] == offsets[:, None]

    def one_target(running, target_seq):
        group_base = (target_seq // NDOC) * NDOC
        target = target_seq % NDOC
        sources = (group_base + doc_ids).astype(jnp.int32)
        chosen = inverse[sources, target]
        length = doc_lengths[sources, chosen]
        first_tok = starts[sources, chosen]
        filled = offsets[None, :] < length[:, None]
        position = jnp.minimum(first_tok[:, None] + offsets[None, :], L - 1).astype(jnp.int32)

        def gather_rows(source):
            picked = source[sources[:, None], position]
            return jnp.where(filled[:, :, None], picked, jnp.zeros((), source.dtype))

        query_recv = gather_rows(queries).astype(jnp.float32).reshape(NDOC, CAP, KVH, group_size, HD)
        key_recv = gather_rows(key_rows).astype(jnp.float32).reshape(NDOC, CAP, KVH, HD)
        value_recv = gather_rows(value_rows).astype(jnp.float32).reshape(NDOC, CAP, KVH, HD)
        grad_recv = gather_rows(out_grad).astype(jnp.float32).reshape(NDOC, CAP, KVH, group_size, HD)
        allowed = (causal[None] & (filled[:, :, None] | diagonal[None])).astype(jnp.int32)
        query_grad, key_grad, value_grad = block_grads(query_recv, key_recv, value_recv, grad_recv, allowed)
        query_out = query_grad.reshape(RECV, HEADS * HD).astype(jnp.bfloat16)
        key_out = key_grad.reshape(RECV, KVH * HD).astype(jnp.bfloat16)
        value_out = value_grad.reshape(RECV, KVH * HD).astype(jnp.bfloat16)
        input_recv = gather_rows(inputs).reshape(RECV, D).astype(jnp.float32)
        running = running + jnp.dot(input_recv.T, value_out.astype(jnp.float32), precision=lax.Precision.HIGHEST)
        return running, (query_out, key_out, value_out)

    summed, outputs = lax.scan(one_target, jnp.zeros((D, KVH * HD), jnp.float32), jnp.arange(SEQS, dtype=jnp.int32))
    return outputs[0], outputs[1], outputs[2], summed
```

```python
import functools

import jax
import jax.numpy as jnp
from jax import lax
from jax.experimental import pallas as pl
from jax.experimental.pallas import tpu as pltpu
from jax.sharding import PartitionSpec as P

HEADS = 32
KVH = 8
HD = 128
MESH = pl.DeviceIdType.MESH
F32 = jnp.float32
BF16 = jnp.bfloat16


def dot(a, b, ca, cb):
    return lax.dot_general(a, b, (((ca,), (cb,)), ((), ())), preferred_element_type=F32)


def attend_kernel(first_ref, len_ref, q_ref, k_ref, v_ref, g_ref, dq_ref, dk_ref, dv_ref, tok_ref, acc):
    n_blocks, cap = dq_ref.shape[0], dq_ref.shape[1]
    seq_len = q_ref.shape[0]
    kv_local = k_ref.shape[1] // HD
    group = HEADS // KVH
    scale = HD ** (-0.5)
    acc[...] = jnp.zeros_like(acc)

    def block(i, carry):
        first, length = first_ref[i], len_ref[i]
        row = lax.broadcasted_iota(jnp.int32, (cap, seq_len), 0)
        token = lax.broadcasted_iota(jnp.int32, (cap, seq_len), 1)
        pick = jnp.where((token == first + row) & (row < length), 1.0, 0.0).astype(BF16)
        row_t = lax.broadcasted_iota(jnp.int32, (seq_len, cap), 1)
        token_t = lax.broadcasted_iota(jnp.int32, (seq_len, cap), 0)
        place = jnp.where((token_t == first + row_t) & (row_t < length), 1.0, 0.0).astype(BF16)
        r = lax.broadcasted_iota(jnp.int32, (cap, cap), 0)
        c = lax.broadcasted_iota(jnp.int32, (cap, cap), 1)
        allowed = (c <= r) & ((r < length) | (c == r))
        allowed = jnp.concatenate([allowed.astype(F32)] * group, axis=0) > 0.5
        for n in range(kv_local):
            kv = slice(n * HD, (n + 1) * HD)
            wide = slice(n * group * HD, (n + 1) * group * HD)
            kb = dot(pick, k_ref[:, kv], 1, 0).astype(BF16)
            vb = dot(pick, v_ref[:, kv], 1, 0).astype(BF16)
            qw = dot(pick, q_ref[:, wide], 1, 0).astype(BF16)
            gw = dot(pick, g_ref[:, wide], 1, 0).astype(BF16)
            qb = jnp.concatenate([qw[:, h * HD:(h + 1) * HD] for h in range(group)], axis=0)
            gb = jnp.concatenate([gw[:, h * HD:(h + 1) * HD] for h in range(group)], axis=0)
            scores = jnp.where(allowed, dot(qb, kb, 1, 1) * scale, -jnp.inf)
            raised = jnp.exp(scores - jnp.max(scores, axis=1, keepdims=True))
            probs = raised / jnp.sum(raised, axis=1, keepdims=True)
            low = probs.astype(BF16)
            prob_grad = dot(gb, vb, 1, 1)
            delta = jnp.sum(low.astype(F32) * prob_grad, axis=1, keepdims=True)
            dscore = (probs * (prob_grad - delta)).astype(BF16)
            dq = (dot(dscore, kb, 1, 0) * scale).astype(BF16)
            for h in range(group):
                at = (n * group + h) * HD
                dq_ref[i, :, at:at + HD] = dq[h * cap:(h + 1) * cap]
            dk_ref[i, :, kv] = (dot(dscore, qb, 0, 0) * scale).astype(BF16)
            dv = dot(low, gb, 0, 0).astype(BF16)
            dv_ref[i, :, kv] = dv
            acc[:, kv] += dot(place, dv, 1, 0)
        return carry

    lax.fori_loop(0, n_blocks, block, 0)
    tok_ref[...] = acc[...].astype(BF16)


def exchange_kernel(
    n_dp, n_ctx, n_tp,
    dq_ref, dk_ref, dv_ref, tok_ref, x_ref,
    q_out, k_out, v_out, w_out,
    xt, vals, a_send, a_recv, keep, b_send, b_recv, c_send, c_recv,
    own_sem, ctx_ssem, ctx_rsem, z_ssem, z_rsem, a_ssem, a_rsem, b_ssem, b_rsem, c_ssem, c_rsem,
):
    dp, ctx, tp = lax.axis_index("dp"), lax.axis_index("ctx"), lax.axis_index("tp")
    n_far = n_ctx // 2
    far, near = ctx // 2, ctx % 2
    rows, width = keep.shape[3], keep.shape[4]

    def ctx_at(p):
        return (dp, lax.rem(ctx + p, n_ctx), tp)

    def tp_at(p):
        return (dp, ctx, lax.rem(tp + p, n_tp))

    def dp_at(p):
        return (lax.rem(dp + p, n_dp), ctx, tp)

    barrier = pltpu.get_barrier_semaphore()
    for p in range(1, n_ctx):
        pl.semaphore_signal(barrier, inc=1, device_id=ctx_at(p), device_id_type=MESH)
    for p in range(1, n_tp):
        pl.semaphore_signal(barrier, inc=1, device_id=tp_at(p), device_id_type=MESH)
    for p in range(1, n_dp):
        pl.semaphore_signal(barrier, inc=1, device_id=dp_at(p), device_id_type=MESH)
    pl.semaphore_wait(barrier, n_ctx + n_tp + n_dp - 3)

    def remote(src, dst, ssem, rsem, device):
        return pltpu.make_async_remote_copy(
            src_ref=src, dst_ref=dst, send_sem=ssem, recv_sem=rsem,
            device_id=device, device_id_type=MESH)

    order = [0]
    for p in range(1, n_tp // 2 + 1):
        order += [p] if 2 * p == n_tp else [p, n_tp - p]
    gathers = {}
    for p in order[1:]:
        gathers[p] = remote(tok_ref, vals.at[p], z_ssem.at[p], z_rsem.at[p], tp_at(p))
        gathers[p].start()
    moves = []
    for p in range(1, n_ctx):
        dest = lax.rem(ctx + p, n_ctx)
        for t, (src, dst) in enumerate(((dq_ref, q_out), (dk_ref, k_out), (dv_ref, v_out))):
            move = remote(src.at[dest], dst.at[ctx], ctx_ssem.at[t, p], ctx_rsem.at[t, p], ctx_at(p))
            move.start()
            moves.append(move)
    owns = []
    for t, (src, dst) in enumerate(((dq_ref, q_out), (dk_ref, k_out), (dv_ref, v_out))):
        own = pltpu.make_async_copy(src.at[ctx], dst.at[ctx], own_sem.at[t])
        own.start()
        owns.append(own)

    for b in range(n_dp * n_ctx):
        xt[b] = x_ref[:, b * rows:(b + 1) * rows].T

    near_copies, dp_copies, far_copies = {}, {}, {}
    partner = (dp, far * 2 + 1 - near, tp)

    def stage_near(u):
        p = order[u]
        if p:
            gathers[p].wait_recv()
        block = tok_ref[...] if p == 0 else vals[p]
        for d in range(n_dp):
            for f in range(n_far):
                a_send[u, d, f] = dot(xt[d * n_ctx + f * 2 + 1 - near], block, 1, 0).astype(BF16)
        near_copies[u] = remote(a_send.at[u], a_recv.at[u], a_ssem.at[u], a_rsem.at[u], partner)
        near_copies[u].start()
        for d in range(n_dp):
            for f in range(n_far):
                keep[u, d, f] = dot(xt[d * n_ctx + f * 2 + near], block, 1, 0)

    def stage_dp(u):
        near_copies[u].wait_recv()
        dp_copies[u] = []
        for p in range(1, n_dp):
            dest = lax.rem(dp + p, n_dp)
            b_send[u, p] = (keep[u, dest] + a_recv[u, dest].astype(F32)).astype(BF16)
            copy = remote(b_send.at[u, p], b_recv.at[u, p], b_ssem.at[u, p], b_rsem.at[u, p], dp_at(p))
            copy.start()
            dp_copies[u].append(copy)
        keep[u, dp] += a_recv[u, dp].astype(F32)

    def stage_far(u):
        for copy in dp_copies[u]:
            copy.wait_recv()
        far_copies[u] = []
        for p in range(1, n_far):
            dest = lax.rem(far + p, n_far)
            total = keep[u, dp, dest]
            for s in range(1, n_dp):
                total += b_recv[u, s, dest].astype(F32)
            c_send[u, p] = total.astype(BF16)
            copy = remote(
                c_send.at[u, p], c_recv.at[u, p], c_ssem.at[u, p], c_rsem.at[u, p],
                (dp, dest * 2 + near, tp))
            copy.start()
            far_copies[u].append(copy)

    def stage_last(u):
        for copy in far_copies[u]:
            copy.wait_recv()
        total = keep[u, dp, far]
        for s in range(1, n_dp):
            total += b_recv[u, s, far].astype(F32)
        for s in range(1, n_far):
            total += c_recv[u, s].astype(F32)
        source = lax.rem(tp + n_tp - order[u], n_tp)
        w_out[:, pl.ds(pl.multiple_of(source * width, width), width)] = total

    for u in range(n_tp + 3):
        for lag, stage in ((3, stage_last), (2, stage_far), (1, stage_dp), (0, stage_near)):
            if 0 <= u - lag < n_tp:
                stage(u - lag)

    for own in owns:
        own.wait()
    for move in moves:
        move.wait()
    for p in order[1:]:
        gathers[p].wait_send()
    for u in range(n_tp):
        near_copies[u].wait_send()
        for copy in dp_copies[u] + far_copies[u]:
            copy.wait_send()


def shards(queries, key_rows, value_rows, out_grad, inputs, doc_lengths, doc_plan):
    n_dp, n_ctx, n_tp = (lax.axis_size(a) for a in ("dp", "ctx", "tp"))
    own_index = lax.axis_index("ctx")
    seq_len = queries.shape[1]
    capacity = 5 * seq_len // (4 * n_ctx)
    padded = -(-capacity // 16) * 16
    q_width, kv_width, features = queries.shape[2], key_rows.shape[2], inputs.shape[2]
    n_far = n_ctx // 2
    rows = features // (n_dp * n_ctx)

    doc_ids = jnp.arange(n_ctx, dtype=jnp.int32)
    lengths = lax.dynamic_index_in_dim(doc_lengths, own_index, 0, keepdims=False)
    plan = lax.dynamic_index_in_dim(doc_plan, own_index, 0, keepdims=False)
    starts = jnp.sum(jnp.where(doc_ids[None, :] < doc_ids[:, None], lengths[None, :], 0), axis=1)
    chosen = plan[None, :] == doc_ids[:, None]
    send_len = jnp.sum(jnp.where(chosen, lengths[None, :], 0), axis=1)
    send_first = jnp.sum(jnp.where(chosen, starts[None, :], 0), axis=1)

    vmem = pl.BlockSpec(memory_space=pltpu.VMEM)
    smem = pl.BlockSpec(memory_space=pltpu.SMEM)
    anywhere = pl.BlockSpec(memory_space=pl.ANY)
    dq, dk, dv, tok = pl.pallas_call(
        attend_kernel,
        out_shape=(
            jax.ShapeDtypeStruct((n_ctx, padded, q_width), BF16),
            jax.ShapeDtypeStruct((n_ctx, padded, kv_width), BF16),
            jax.ShapeDtypeStruct((n_ctx, padded, kv_width), BF16),
            jax.ShapeDtypeStruct((seq_len, kv_width), BF16),
        ),
        in_specs=[smem, smem, vmem, vmem, vmem, vmem],
        out_specs=(vmem, vmem, vmem, vmem),
        scratch_shapes=[pltpu.VMEM((seq_len, kv_width), F32)],
        compiler_params=pltpu.CompilerParams(vmem_limit_bytes=32 << 20),
        name="attend",
    )(send_first, send_len, queries[0], key_rows[0], value_rows[0], out_grad[0])

    dma = pltpu.SemaphoreType.DMA
    q_out, k_out, v_out, w_out = pl.pallas_call(
        functools.partial(exchange_kernel, n_dp, n_ctx, n_tp),
        out_shape=(
            jax.ShapeDtypeStruct(dq.shape, BF16),
            jax.ShapeDtypeStruct(dk.shape, BF16),
            jax.ShapeDtypeStruct(dv.shape, BF16),
            jax.ShapeDtypeStruct((rows, n_tp * kv_width), F32),
        ),
        in_specs=[anywhere, anywhere, anywhere, vmem, vmem],
        out_specs=(anywhere, anywhere, anywhere, vmem),
        scratch_shapes=[
            pltpu.VMEM((n_dp * n_ctx, rows, seq_len), BF16),
            pltpu.VMEM((n_tp, seq_len, kv_width), BF16),
            pltpu.VMEM((n_tp, n_dp, n_far, rows, kv_width), BF16),
            pltpu.VMEM((n_tp, n_dp, n_far, rows, kv_width), BF16),
            pltpu.VMEM((n_tp, n_dp, n_far, rows, kv_width), F32),
            pltpu.VMEM((n_tp, n_dp, n_far, rows, kv_width), BF16),
            pltpu.VMEM((n_tp, n_dp, n_far, rows, kv_width), BF16),
            pltpu.VMEM((n_tp, n_far, rows, kv_width), BF16),
            pltpu.VMEM((n_tp, n_far, rows, kv_width), BF16),
            dma((3,)),
            dma((3, n_ctx)), dma((3, n_ctx)),
            dma((n_tp,)), dma((n_tp,)),
            dma((n_tp,)), dma((n_tp,)),
            dma((n_tp, n_dp)), dma((n_tp, n_dp)),
            dma((n_tp, n_far)), dma((n_tp, n_far)),
        ],
        compiler_params=pltpu.CompilerParams(
            collective_id=0, has_side_effects=True, vmem_limit_bytes=40 << 20),
        name="exchange",
    )(dq, dk, dv, tok, inputs[0])

    def joined(block):
        return block[:, :capacity].reshape(1, n_ctx * capacity, block.shape[2])

    return joined(q_out), joined(k_out), joined(v_out), w_out


def solution(mesh):
    rows_placed = P(("dp", "ctx"), None, "tp")
    return jax.shard_map(
        shards,
        mesh=mesh,
        in_specs=(rows_placed,) * 5 + (P("dp", None),) * 2,
        out_specs=(rows_placed, rows_placed, rows_placed, P(("tp", "dp", "ctx"), None)),
        check_vma=False,
    )
```

```python
import functools

import jax
import jax.numpy as jnp
from jax import lax
from jax.experimental import pallas as pl
from jax.experimental.pallas import tpu as pltpu
from jax.sharding import PartitionSpec as P

HEADS = 32
KVH = 8
HD = 128
MESH = pl.DeviceIdType.MESH
F32 = jnp.float32
BF16 = jnp.bfloat16


def dot(a, b, ca, cb):
    return lax.dot_general(a, b, (((ca,), (cb,)), ((), ())), preferred_element_type=F32)


def fused_kernel(
    n_dp, n_ctx, n_tp,
    first_ref, len_ref, q_hbm, k_hbm, v_hbm, g_hbm, x_hbm,
    q_out, k_out, v_out, w_out,
    q_ref, k_ref, v_ref, g_ref, x_ref,
    probs_s, qb_s, gb_s, kb_s, vb_s, dq_ref, dk_ref, dv_ref, acc, tok_ref,
    xt, vals, a_send, a_recv, keep, b_send, b_recv, c_send, c_recv,
    in_sem, own_sem, ctx_ssem, ctx_rsem, z_ssem, z_rsem, a_ssem, a_rsem, b_ssem, b_rsem, c_ssem, c_rsem,
):
    dp, ctx, tp = lax.axis_index("dp"), lax.axis_index("ctx"), lax.axis_index("tp")
    n_far = n_ctx // 2
    far, near = ctx // 2, ctx % 2
    rows, width = keep.shape[3], keep.shape[4]

    def ctx_at(p):
        return (dp, lax.rem(ctx + p, n_ctx), tp)

    def tp_at(p):
        return (dp, ctx, lax.rem(tp + p, n_tp))

    def dp_at(p):
        return (lax.rem(dp + p, n_dp), ctx, tp)

    loads = [
        pltpu.make_async_copy(src, dst, in_sem.at[t])
        for t, (src, dst) in enumerate(
            ((k_hbm, k_ref), (q_hbm, q_ref), (v_hbm, v_ref), (g_hbm, g_ref), (x_hbm, x_ref)))
    ]
    for load in loads:
        load.start()

    barrier = pltpu.get_barrier_semaphore()
    for p in range(1, n_ctx):
        pl.semaphore_signal(barrier, inc=1, device_id=ctx_at(p), device_id_type=MESH)
    for p in range(1, n_tp):
        pl.semaphore_signal(barrier, inc=1, device_id=tp_at(p), device_id_type=MESH)
    for p in range(1, n_dp):
        pl.semaphore_signal(barrier, inc=1, device_id=dp_at(p), device_id_type=MESH)

    cap, seq_len = dq_ref.shape[1], q_ref.shape[0]
    kv_local = k_ref.shape[1] // HD
    group = HEADS // KVH
    scale = HD ** (-0.5)
    acc[...] = jnp.zeros_like(acc)
    for load in loads[:4]:
        load.wait()

    def value_part(i, carry):
        first, length = first_ref[i], len_ref[i]
        row = lax.broadcasted_iota(jnp.int32, (cap, seq_len), 0)
        token = lax.broadcasted_iota(jnp.int32, (cap, seq_len), 1)
        pick = jnp.where((token == first + row) & (row < length), 1.0, 0.0).astype(BF16)
        row_t = lax.broadcasted_iota(jnp.int32, (seq_len, cap), 1)
        token_t = lax.broadcasted_iota(jnp.int32, (seq_len, cap), 0)
        place = jnp.where((token_t == first + row_t) & (row_t < length), 1.0, 0.0).astype(BF16)
        r = lax.broadcasted_iota(jnp.int32, (cap, cap), 0)
        c = lax.broadcasted_iota(jnp.int32, (cap, cap), 1)
        allowed = (c <= r) & ((r < length) | (c == r))
        allowed = jnp.concatenate([allowed.astype(F32)] * group, axis=0) > 0.5
        for n in range(kv_local):
            kv = slice(n * HD, (n + 1) * HD)
            wide = slice(n * group * HD, (n + 1) * group * HD)
            kb = dot(pick, k_ref[:, kv], 1, 0).astype(BF16)
            qw = dot(pick, q_ref[:, wide], 1, 0).astype(BF16)
            gw = dot(pick, g_ref[:, wide], 1, 0).astype(BF16)
            qb = jnp.concatenate([qw[:, h * HD:(h + 1) * HD] for h in range(group)], axis=0)
            gb = jnp.concatenate([gw[:, h * HD:(h + 1) * HD] for h in range(group)], axis=0)
            scores = jnp.where(allowed, dot(qb, kb, 1, 1) * scale, -jnp.inf)
            raised = jnp.exp(scores - jnp.max(scores, axis=1, keepdims=True))
            probs = raised / jnp.sum(raised, axis=1, keepdims=True)
            dv = dot(probs.astype(BF16), gb, 0, 0).astype(BF16)
            dv_ref[i, :, kv] = dv
            acc[:, kv] += dot(place, dv, 1, 0)
            vb_s[i, n] = dot(pick, v_ref[:, kv], 1, 0).astype(BF16)
            probs_s[i, n] = probs
            qb_s[i, n] = qb
            gb_s[i, n] = gb
            kb_s[i, n] = kb
        return carry

    lax.fori_loop(0, n_ctx, value_part, 0)
    tok_ref[...] = acc[...].astype(BF16)

    def query_key_part(i):
        for n in range(kv_local):
            kv = slice(n * HD, (n + 1) * HD)
            probs = probs_s[i, n]
            kb = kb_s[i, n]
            prob_grad = dot(gb_s[i, n], vb_s[i, n], 1, 1)
            low = probs.astype(BF16).astype(F32)
            delta = jnp.sum(low * prob_grad, axis=1, keepdims=True)
            dscore = (probs * (prob_grad - delta)).astype(BF16)
            dq = (dot(dscore, kb, 1, 0) * scale).astype(BF16)
            for h in range(group):
                at = (n * group + h) * HD
                dq_ref[i, :, at:at + HD] = dq[h * cap:(h + 1) * cap]
            dk_ref[i, :, kv] = (dot(dscore, qb_s[i, n], 0, 0) * scale).astype(BF16)

    pl.semaphore_wait(barrier, n_ctx + n_tp + n_dp - 3)

    def remote(src, dst, ssem, rsem, device):
        return pltpu.make_async_remote_copy(
            src_ref=src, dst_ref=dst, send_sem=ssem, recv_sem=rsem,
            device_id=device, device_id_type=MESH)

    order = [0]
    for p in range(1, n_tp // 2 + 1):
        order += [p] if 2 * p == n_tp else [p, n_tp - p]
    gathers = {}
    for p in order[1:]:
        gathers[p] = remote(tok_ref, vals.at[p], z_ssem.at[p], z_rsem.at[p], tp_at(p))
        gathers[p].start()
    def move(t, p):
        src, dst = ((dq_ref, q_out), (dk_ref, k_out), (dv_ref, v_out))[t]
        dest = lax.rem(ctx + p, n_ctx)
        return remote(src.at[dest], dst.at[ctx], ctx_ssem.at[t, p], ctx_rsem.at[t, p], ctx_at(p))

    def own(t):
        src, dst = ((dq_ref, q_out), (dk_ref, k_out), (dv_ref, v_out))[t]
        return pltpu.make_async_copy(src.at[ctx], dst.at[ctx], own_sem.at[t])

    def send_block(p, carry):
        query_key_part(lax.rem(ctx + p, n_ctx))
        for t in range(3):
            move(t, p).start()
        return carry

    lax.fori_loop(1, n_ctx, send_block, 0)
    loads[4].wait()
    for b in range(n_dp * n_ctx):
        xt[b] = x_ref[:, b * rows:(b + 1) * rows].T

    near_copies, dp_copies, far_copies = {}, {}, {}
    partner = (dp, far * 2 + 1 - near, tp)

    def stage_near(u):
        p = order[u]
        if p:
            gathers[p].wait_recv()
        block = tok_ref[...] if p == 0 else vals[p]
        for d in range(n_dp):
            for f in range(n_far):
                a_send[u, d, f] = dot(xt[d * n_ctx + f * 2 + 1 - near], block, 1, 0).astype(BF16)
        near_copies[u] = remote(a_send.at[u], a_recv.at[u], a_ssem.at[u], a_rsem.at[u], partner)
        near_copies[u].start()
        for d in range(n_dp):
            for f in range(n_far):
                keep[u, d, f] = dot(xt[d * n_ctx + f * 2 + near], block, 1, 0)

    def stage_dp(u):
        near_copies[u].wait_recv()
        dp_copies[u] = []
        for p in range(1, n_dp):
            dest = lax.rem(dp + p, n_dp)
            b_send[u, p] = (keep[u, dest] + a_recv[u, dest].astype(F32)).astype(BF16)
            copy = remote(b_send.at[u, p], b_recv.at[u, p], b_ssem.at[u, p], b_rsem.at[u, p], dp_at(p))
            copy.start()
            dp_copies[u].append(copy)
        keep[u, dp] += a_recv[u, dp].astype(F32)

    def stage_far(u):
        for copy in dp_copies[u]:
            copy.wait_recv()
        far_copies[u] = []
        for p in range(1, n_far):
            dest = lax.rem(far + p, n_far)
            total = keep[u, dp, dest]
            for s in range(1, n_dp):
                total += b_recv[u, s, dest].astype(F32)
            c_send[u, p] = total.astype(BF16)
            copy = remote(
                c_send.at[u, p], c_recv.at[u, p], c_ssem.at[u, p], c_rsem.at[u, p],
                (dp, dest * 2 + near, tp))
            copy.start()
            far_copies[u].append(copy)

    def stage_last(u):
        for copy in far_copies[u]:
            copy.wait_recv()
        total = keep[u, dp, far]
        for s in range(1, n_dp):
            total += b_recv[u, s, far].astype(F32)
        for s in range(1, n_far):
            total += c_recv[u, s].astype(F32)
        source = lax.rem(tp + n_tp - order[u], n_tp)
        w_out[:, pl.ds(pl.multiple_of(source * width, width), width)] = total

    for u in range(n_tp + 3):
        for lag, stage in ((3, stage_last), (2, stage_far), (1, stage_dp), (0, stage_near)):
            if 0 <= u - lag < n_tp:
                stage(u - lag)
        if u == 0:
            query_key_part(ctx)
            for t in range(3):
                own(t).start()

    for t in range(3):
        own(t).wait()
        for p in range(1, n_ctx):
            move(t, p).wait()
    for p in order[1:]:
        gathers[p].wait_send()
    for u in range(n_tp):
        near_copies[u].wait_send()
        for copy in dp_copies[u] + far_copies[u]:
            copy.wait_send()


def shards(queries, key_rows, value_rows, out_grad, inputs, doc_lengths, doc_plan):
    n_dp, n_ctx, n_tp = (lax.axis_size(a) for a in ("dp", "ctx", "tp"))
    own_index = lax.axis_index("ctx")
    seq_len = queries.shape[1]
    capacity = 5 * seq_len // (4 * n_ctx)
    padded = -(-capacity // 16) * 16
    q_width, kv_width, features = queries.shape[2], key_rows.shape[2], inputs.shape[2]
    n_far = n_ctx // 2
    rows = features // (n_dp * n_ctx)

    doc_ids = jnp.arange(n_ctx, dtype=jnp.int32)
    lengths = lax.dynamic_index_in_dim(doc_lengths, own_index, 0, keepdims=False)
    plan = lax.dynamic_index_in_dim(doc_plan, own_index, 0, keepdims=False)
    starts = jnp.sum(jnp.where(doc_ids[None, :] < doc_ids[:, None], lengths[None, :], 0), axis=1)
    chosen = plan[None, :] == doc_ids[:, None]
    send_len = jnp.sum(jnp.where(chosen, lengths[None, :], 0), axis=1)
    send_first = jnp.sum(jnp.where(chosen, starts[None, :], 0), axis=1)

    kv_local = kv_width // HD
    stacked = HEADS // KVH * padded
    vmem = pl.BlockSpec(memory_space=pltpu.VMEM)
    smem = pl.BlockSpec(memory_space=pltpu.SMEM)
    anywhere = pl.BlockSpec(memory_space=pl.ANY)
    dma = pltpu.SemaphoreType.DMA
    q_out, k_out, v_out, w_out = pl.pallas_call(
        functools.partial(fused_kernel, n_dp, n_ctx, n_tp),
        out_shape=(
            jax.ShapeDtypeStruct((n_ctx, padded, q_width), BF16),
            jax.ShapeDtypeStruct((n_ctx, padded, kv_width), BF16),
            jax.ShapeDtypeStruct((n_ctx, padded, kv_width), BF16),
            jax.ShapeDtypeStruct((rows, n_tp * kv_width), F32),
        ),
        in_specs=[smem, smem] + [anywhere] * 5,
        out_specs=(anywhere, anywhere, anywhere, vmem),
        scratch_shapes=[
            pltpu.VMEM((seq_len, q_width), BF16),
            pltpu.VMEM((seq_len, kv_width), BF16),
            pltpu.VMEM((seq_len, kv_width), BF16),
            pltpu.VMEM((seq_len, q_width), BF16),
            pltpu.VMEM((seq_len, features), BF16),
            pltpu.VMEM((n_ctx, kv_local, stacked, padded), F32),
            pltpu.VMEM((n_ctx, kv_local, stacked, HD), BF16),
            pltpu.VMEM((n_ctx, kv_local, stacked, HD), BF16),
            pltpu.VMEM((n_ctx, kv_local, padded, HD), BF16),
            pltpu.VMEM((n_ctx, kv_local, padded, HD), BF16),
            pltpu.VMEM((n_ctx, padded, q_width), BF16),
            pltpu.VMEM((n_ctx, padded, kv_width), BF16),
            pltpu.VMEM((n_ctx, padded, kv_width), BF16),
            pltpu.VMEM((seq_len, kv_width), F32),
            pltpu.VMEM((seq_len, kv_width), BF16),
            pltpu.VMEM((n_dp * n_ctx, rows, seq_len), BF16),
            pltpu.VMEM((n_tp, seq_len, kv_width), BF16),
            pltpu.VMEM((n_tp, n_dp, n_far, rows, kv_width), BF16),
            pltpu.VMEM((n_tp, n_dp, n_far, rows, kv_width), BF16),
            pltpu.VMEM((n_tp, n_dp, n_far, rows, kv_width), F32),
            pltpu.VMEM((n_tp, n_dp, n_far, rows, kv_width), BF16),
            pltpu.VMEM((n_tp, n_dp, n_far, rows, kv_width), BF16),
            pltpu.VMEM((n_tp, n_far, rows, kv_width), BF16),
            pltpu.VMEM((n_tp, n_far, rows, kv_width), BF16),
            dma((5,)),
            dma((3,)),
            dma((3, n_ctx)), dma((3, n_ctx)),
            dma((n_tp,)), dma((n_tp,)),
            dma((n_tp,)), dma((n_tp,)),
            dma((n_tp, n_dp)), dma((n_tp, n_dp)),
            dma((n_tp, n_far)), dma((n_tp, n_far)),
        ],
        compiler_params=pltpu.CompilerParams(
            collective_id=0, has_side_effects=True, vmem_limit_bytes=56 << 20),
        name="fused",
    )(send_first, send_len, queries[0], key_rows[0], value_rows[0], out_grad[0], inputs[0])

    def joined(block):
        return block[:, :capacity].reshape(1, n_ctx * capacity, block.shape[2])

    return joined(q_out), joined(k_out), joined(v_out), w_out


def solution(mesh):
    rows_placed = P(("dp", "ctx"), None, "tp")
    return jax.shard_map(
        shards,
        mesh=mesh,
        in_specs=(rows_placed,) * 5 + (P("dp", None),) * 2,
        out_specs=(rows_placed, rows_placed, rows_placed, P(("tp", "dp", "ctx"), None)),
        check_vma=False,
    )
```
